32 devices in a mesh: slide: 8 (over z, x), ctx: 4 (over y, core).
Axes of the slice: x: 2, y: 2, z: 4, core: 2. Of those that a mesh axis runs over, the one named last changes fastest.
Arguments:
- feature_maps: bfloat16 [1024, 16, 16, 384], P(('slide', 'ctx')), may hold values from -6 to 6
- down_weight: bfloat16 [1536, 768], replicated, may hold values from -0.15625 to 0.15625
- conv_taps: bfloat16 [49, 768], replicated, may hold values from -0.875 to 0.875
- mlp_in: bfloat16 [768, 3072], replicated, may hold values from -0.21875 to 0.21875
- mlp_out: bfloat16 [3072, 768], replicated, may hold values from -0.109375 to 0.109375
- layer_scale: float32 [768], replicated, may hold values from 0.2 to 1
- qkv_weight: bfloat16 [1, 768, 2304], replicated, may hold values from -4.690971 to 4.690971
- out_weight: bfloat16 [1, 768, 768], replicated, may hold values from -0.21875 to 0.21875
- tile_slide: int32 [1024], P(('slide', 'ctx')), may hold values from 0 to 7, as said below
- tile_pos: int32 [1024], P(('slide', 'ctx')), may hold values from 0 to 767, as said below
- slide_len: int32 [8], replicated, may hold values from 1 to 768, as said below
Outputs:
- slide_tokens: bfloat16 [6144, 768], P(('slide', 'ctx'))
The draws below stay inside these ranges and needn't reach their ends.
Inputs may be any that keep to these rules, and one draw needn't show every extreme that they name: `tile_slide`: the tiles of slide s lie at positions 0 to slide_len[s] - 1 of it, exactly one tile at each. `tile_pos`: among the tiles of one device at most 6 lie in the same block of 192 positions of one slide, and some device has exactly 6 in some block. `slide_len`: the lengths sum to 1024; some slide has exactly 768 tiles.
All inputs are finite; a program needn't handle non-finite values.
Results may differ from the reference program's by a relative error of at most 0.015.
Values may be sent and summed in bfloat16 or wider, within the bound.
No kernel may reach another device: no remote copies, remote signals or barrier semaphores. Data moves between devices by JAX's collectives and lax.ppermute only.
A program may use at most 128 MiB of HBM per device.

```python
import math
import jax
import jax.numpy as jnp
from jax import lax

C_IN = 384
D = 768
MLP_DIM = 3072
HEADS = 12
HEAD_DIM = 64
MAP = 16
KS = 7
LAYERS = 1
TILES_DEV = 32
SLIDES = 8
SEQ = 768
TILES = 1024
SLOTS = 6144


def tile_layout(key):
    layout_key = jax.random.fold_in(key, 7)
    lead_key, pair_key, order_key, source_key, local_key = jax.random.split(layout_key, 5)
    mean_len = TILES // SLIDES
    rest_sum = 8 * mean_len - SEQ
    part_sum = rest_sum // 4
    lead_cuts = jax.random.randint(lead_key, (3,), 1, part_sum, dtype=jnp.int32)
    leading = jnp.concatenate([jnp.full((1,), SEQ, jnp.int32), lead_cuts, part_sum - lead_cuts, jnp.full((1,), rest_sum - 3 * part_sum, jnp.int32)]).astype(jnp.int32)
    paired = jax.random.randint(pair_key, ((SLIDES - 8) // 2,), 1, 2 * mean_len, dtype=jnp.int32)
    lengths = jnp.concatenate([leading, paired, 2 * mean_len - paired]).astype(jnp.int32)
    lengths = lengths[jax.random.permutation(order_key, SLIDES)]
    starts = (jnp.cumsum(lengths) - lengths).astype(jnp.int32)
    flat_index = jnp.arange(TILES, dtype=jnp.int32)
    slide_of = jnp.sum((starts[None, :] <= flat_index[:, None]).astype(jnp.int32), axis=1) - 1
    place_of = flat_index - starts[slide_of]
    device_total = TILES // TILES_DEV
    source_order = jax.random.permutation(source_key, device_total).astype(jnp.int32)
    local_order = jax.random.permutation(local_key, TILES_DEV).astype(jnp.int32)
    landing = source_order[flat_index % device_total] * TILES_DEV + local_order[flat_index // device_total]
    slide_list = jnp.zeros((TILES,), jnp.int32).at[landing].set(slide_of.astype(jnp.int32))
    place_list = jnp.zeros((TILES,), jnp.int32).at[landing].set(place_of.astype(jnp.int32))
    return (slide_list, place_list, lengths)


def draw_tile_slide(key, part):
    return tile_layout(key)[0]


def draw_tile_pos(key, part):
    return tile_layout(key)[1]


def draw_slide_len(key, part):
    return tile_layout(key)[2]


def draw_qkv_weight(key, part):
    base_key = jax.random.fold_in(jax.random.fold_in(key, 11), 0)
    matrix = jax.random.truncated_normal(base_key, -4.0, 4.0, (LAYERS, D, 3 * D), jnp.float32) * D ** (-0.5)
    return matrix.astype(jnp.bfloat16)


def block_levels(rng, extent, cuts, smallest, largest):
    level = 1.0
    for position, blocks in cuts:
        heights = jax.random.uniform(jax.random.fold_in(jax.random.fold_in(rng, 6), position), (blocks,), jnp.float32, smallest / len(cuts), largest / len(cuts))
        level = level * jnp.repeat(jnp.exp(heights), extent[position] // blocks).reshape((-1,) + (1,) * (len(extent) - 1 - position))
    return level


def centred(rng, extent, scale, limit, cuts=(), held_as=jnp.bfloat16):
    values = jax.random.normal(rng, extent, jnp.float32) * scale
    if len(cuts) > 0:
        values = block_levels(rng, extent, cuts, -0.22, 0.18) * values
    return jnp.clip(values, min=-limit, max=limit).astype(held_as)


def setup_inputs(seed: int = 0) -> dict:
    arg_keys = jax.random.split(jax.random.key(seed), 12)
    feature_maps = centred(arg_keys[0], (TILES, MAP, MAP, C_IN), 1.0, 6.0, ((0, 32),))
    down_weight = centred(arg_keys[1], (4 * C_IN, D), (4 * C_IN) ** -0.5, 0.15625)
    conv_taps = centred(arg_keys[2], (KS * KS, D), (KS * KS) ** -0.5, 0.875)
    mlp_in = centred(arg_keys[3], (D, MLP_DIM), D ** -0.5, 0.21875)
    mlp_out = centred(arg_keys[4], (MLP_DIM, D), MLP_DIM ** -0.5, 0.109375)
    layer_scale = jnp.clip(jnp.exp(jax.random.uniform(arg_keys[5], (D,), jnp.float32, math.log(0.2), math.log(1.0))), 0.2, 1.0)
    qkv_weight = draw_qkv_weight(jax.random.fold_in(arg_keys[11], 71), 0)
    out_weight = centred(arg_keys[7], (LAYERS, D, D), D ** -0.5, 0.21875)
    tile_slide = draw_tile_slide(jax.random.fold_in(arg_keys[11], 71), 0)
    tile_pos = draw_tile_pos(jax.random.fold_in(arg_keys[11], 71), 0)
    slide_len = draw_slide_len(jax.random.fold_in(arg_keys[11], 71), 0)
    return dict(feature_maps=feature_maps, down_weight=down_weight, conv_taps=conv_taps, mlp_in=mlp_in, mlp_out=mlp_out, layer_scale=layer_scale, qkv_weight=qkv_weight, out_weight=out_weight, tile_slide=tile_slide, tile_pos=tile_pos, slide_len=slide_len)


NORM_EPS = 1e-06
FAR_NEGATIVE = -1e+30

def layer_norm(values):
    center = values - lax.optimization_barrier(jnp.mean(values, axis=-1, keepdims=True))
    spread = lax.optimization_barrier(jnp.mean(center * center, axis=-1, keepdims=True))
    return center * lax.rsqrt(spread + NORM_EPS)

def encode_tiles(tile_maps, down_weight, conv_taps, mlp_in, mlp_out, layer_scale):
    tile_count = tile_maps.shape[0]
    half_side = MAP // 2
    normed = layer_norm(tile_maps.astype(jnp.float32)).astype(jnp.bfloat16)
    patches = normed.reshape(tile_count, half_side, 2, half_side, 2, C_IN).transpose(0, 1, 3, 2, 4, 5)
    patches = patches.reshape(tile_count * half_side * half_side, 4 * C_IN)
    reduced = jnp.dot(patches, down_weight, preferred_element_type=jnp.float32).astype(jnp.bfloat16)
    widened = reduced.reshape(tile_count, half_side, half_side, D).astype(jnp.float32)
    tap_values = conv_taps.astype(jnp.float32)
    pad_reach = KS // 2
    padded = jnp.pad(widened, ((0, 0), (pad_reach, pad_reach), (pad_reach, pad_reach), (0, 0)))
    spatial = jnp.zeros_like(widened)
    for row_off in range(KS):
        for col_off in range(KS):
            spatial = spatial + padded[:, row_off:row_off + half_side, col_off:col_off + half_side, :] * tap_values[row_off * KS + col_off]
    spatial_normed = layer_norm(spatial).astype(jnp.bfloat16).reshape(tile_count * half_side * half_side, D)
    expanded = jax.nn.gelu(jnp.dot(spatial_normed, mlp_in, preferred_element_type=jnp.float32), approximate=False).astype(jnp.bfloat16)
    branch = jnp.dot(expanded, mlp_out, preferred_element_type=jnp.float32)
    blocked = widened + (layer_scale * branch).reshape(tile_count, half_side, half_side, D)
    pooled = lax.optimization_barrier(jnp.mean(blocked, axis=(1, 2)))
    return layer_norm(pooled).astype(jnp.bfloat16)

def attend_slide(slot_rows, length, qkv_weight, out_weight):
    valid = jnp.arange(SEQ, dtype=jnp.int32) < length
    stream = slot_rows.astype(jnp.float32)
    for layer_idx in range(LAYERS):
        lnorm = layer_norm(stream).astype(jnp.bfloat16)
        packed = jnp.dot(lnorm, qkv_weight[layer_idx], preferred_element_type=jnp.float32).astype(jnp.bfloat16)
        queries = packed[:, :D].reshape(SEQ, HEADS, HEAD_DIM).astype(jnp.float32)
        keys_all = packed[:, D:2 * D].reshape(SEQ, HEADS, HEAD_DIM).astype(jnp.float32)
        values_all = packed[:, 2 * D:].reshape(SEQ, HEADS, HEAD_DIM).astype(jnp.float32)
        scores = jnp.einsum('qhe,khe->hqk', queries, keys_all) * HEAD_DIM ** (-0.5)
        scores = jnp.where(valid[None, None, :], scores, FAR_NEGATIVE)
        peak = lax.optimization_barrier(jnp.max(scores, axis=-1, keepdims=True))
        weights = jnp.where(valid[None, None, :], jnp.exp(scores - peak), 0.0)
        denom = lax.optimization_barrier(jnp.sum(weights, axis=-1))
        weights_bf = lax.optimization_barrier(weights.astype(jnp.bfloat16)).astype(jnp.float32)
        attended = jnp.einsum('hqk,khe->qhe', weights_bf, values_all) / jnp.transpose(denom)[:, :, None]
        attended = attended.reshape(SEQ, D).astype(jnp.bfloat16)
        stream = stream + jnp.dot(attended, out_weight[layer_idx], preferred_element_type=jnp.float32)
    return jnp.where(valid[:, None], stream, 0.0).astype(jnp.bfloat16)

def reference(feature_maps, down_weight, conv_taps, mlp_in, mlp_out, layer_scale, qkv_weight, out_weight, tile_slide, tile_pos, slide_len):
    tile_blocks = feature_maps.reshape(TILES // TILES_DEV, TILES_DEV, MAP, MAP, C_IN)
    embeds = lax.map(lambda tile_maps: encode_tiles(tile_maps, down_weight, conv_taps, mlp_in, mlp_out, layer_scale), tile_blocks)
    embeds = embeds.reshape(TILES, D)
    target = (tile_slide * SEQ + tile_pos).astype(jnp.int32)
    slot_table = jnp.zeros((SLOTS, D), jnp.bfloat16).at[target].set(embeds)
    outputs = lax.map(lambda pair: attend_slide(pair[0], pair[1], qkv_weight, out_weight), (slot_table.reshape(SLIDES, SEQ, D), slide_len))
    return outputs.reshape(SLOTS, D)
```

```python
import functools

import jax
import jax.numpy as jnp
import numpy as np
from jax import lax
from jax.experimental import pallas as pl
from jax.experimental.pallas import tpu as pltpu
from jax.sharding import PartitionSpec as P

HEADS = 12
HEAD_DIM = 64
KS = 7
SEQ_DEV = 192


NORM_EPS = 1e-06
FAR_NEGATIVE = -1e30


def layer_norm(values):
    center = values - jnp.mean(values, axis=-1, keepdims=True)
    spread = jnp.mean(center * center, axis=-1, keepdims=True)
    return center * lax.rsqrt(spread + NORM_EPS)


F32=jnp.float32; BF=jnp.bfloat16
FREQ=64

def tables(side, ks):
    reach=ks//2; n=side+reach
    half=[(0,0)]+[(0,l) for l in range(1,n//2+1)]+[(k,l) for k in range(1,n//2+1) for l in range(n)]
    k=np.array([a for a,_ in half]); l=np.array([b for _,b in half])
    pos=np.arange(side*side); i,j=pos//side,pos%side
    th=2*np.pi*(np.outer(k,i)+np.outer(l,j))/n
    fwd=np.zeros((2*FREQ,side*side)); fwd[:len(half)]=np.cos(th); fwd[FREQ:FREQ+len(half)]=-np.sin(th)
    a=np.arange(ks*ks)//ks-reach; b=np.arange(ks*ks)%ks-reach
    ph=2*np.pi*(np.outer(k,a)+np.outer(l,b))/n
    s=np.where(np.arange(len(half))==0,1.0,2.0)[:,None]/(n*n)
    tap=np.zeros((2*FREQ,ks*ks)); tap[:len(half)]=s*np.cos(ph); tap[FREQ:FREQ+len(half)]=s*np.sin(ph)
    inv=fwd.T.copy()
    perm=np.zeros((4*side*side,4*side*side))
    for dy in range(2):
        for dx in range(2):
            for ii in range(side):
                for jj in range(side):
                    perm[(dy*2+dx)*side*side+ii*side+jj,(2*ii+dy)*2*side+2*jj+dx]=1
    hi=tap.astype(jnp.bfloat16).astype(np.float64)
    return fwd, inv, np.concatenate([hi,tap-hi]), perm

def rows_norm(x):
    c=x-jnp.mean(x,axis=-1,keepdims=True)
    return c*lax.rsqrt(jnp.mean(c*c,axis=-1,keepdims=True)+NORM_EPS)

def gelu_sum_part(h):
    w=jnp.minimum(h*h, 50.0)
    p=0.7975009723173133+w*(0.03701192786292476-0.000352536613169665*w)
    hv=0.5*h
    return hv+hv*jnp.tanh(h*p)

def kernel(G, side, feat, down, taps, win, wout, scale, fwd, inv, taptab, perm, out,
           patches, red, sn, psum, pool, khat):
    step=pl.program_id(0); steps=pl.num_programs(0)
    S=side*side
    C=feat.shape[-1]; D=down.shape[1]; M=win.shape[1]
    @pl.when(step==0)
    def _():
        t2=jnp.dot(taptab[...],taps[...],preferred_element_type=F32)
        khat[...]=t2[:2*FREQ]+t2[2*FREQ:]
    @pl.loop(0,G)
    def _(t):
        xp=jnp.dot(perm[...],feat[t],preferred_element_type=F32)
        n=rows_norm(xp).astype(BF)
        for q in range(4):
            patches[pl.ds(pl.multiple_of(t*S,S),S), q*C:(q+1)*C]=n[q*S:(q+1)*S]
    red[...]=jnp.dot(patches[...],down[...],preferred_element_type=F32).astype(BF)
    @pl.loop(0,G)
    def _(t):
        rows=pl.ds(pl.multiple_of(t*S,S),S)
        f=jnp.dot(fwd[...],red[rows,:],preferred_element_type=F32)
        pool[pl.ds(step*G+t,1),:]=f[0:1]*(1.0/S)
        fr,fi=f[:FREQ],f[FREQ:]
        kr,ki=khat[:FREQ,:],khat[FREQ:,:]
        g=jnp.concatenate([fr*kr-fi*ki, fr*ki+fi*kr],axis=0).astype(BF)
        sp=jnp.dot(inv[...],g,preferred_element_type=F32)
        sn[rows,:]=rows_norm(sp).astype(BF)
    NC=256
    for c in range(M//NC):
        h=jnp.dot(sn[...],win[:,c*NC:(c+1)*NC],preferred_element_type=F32)
        e=gelu_sum_part(h)
        e=e.reshape(G,S//8,8,NC).sum(axis=1).reshape(G*8,NC)
        psum[pl.ds(pl.multiple_of(step*G*8,G*8),G*8), c*NC:(c+1)*NC]=e.astype(BF)
    @pl.when(step==steps-1)
    def _():
        z=jnp.dot(psum[...],wout[...],preferred_element_type=F32)
        z=z.reshape(z.shape[0]//8,8,D).sum(axis=1)*(1.0/S)
        out[...]=rows_norm(pool[...]+scale[...]*z).astype(BF)

def encode(feature_maps, down, taps, win, wout, scale, G=8):
    T,H,W,C=feature_maps.shape
    side=H//2; S=side*side; D=down.shape[1]; M=win.shape[1]; ks=int(round(taps.shape[0]**.5))
    fwd,inv,tt,perm=tables(side,ks)
    args=(feature_maps.reshape(T,H*W,C),down,taps,win,wout,scale.reshape(1,D),
          jnp.asarray(fwd,BF),jnp.asarray(inv,BF),jnp.asarray(tt,BF),jnp.asarray(perm,BF))
    full=lambda a: pl.BlockSpec(a.shape,lambda s:(0,)*a.ndim,pipeline_mode=pl.Buffered(1))
    return pl.pallas_call(
        functools.partial(kernel,G,side),
        grid=(T//G,),
        in_specs=[pl.BlockSpec((G,H*W,C),lambda s:(s,0,0))]+[full(a) for a in args[1:]],
        out_specs=pl.BlockSpec((T,D),lambda s:(0,0)),
        out_shape=jax.ShapeDtypeStruct((T,D),BF),
        scratch_shapes=[pltpu.VMEM((G*S,4*C),BF),pltpu.VMEM((G*S,D),BF),pltpu.VMEM((G*S,D),BF),
                        pltpu.VMEM((T*8,M),BF),pltpu.VMEM((T,D),F32),pltpu.VMEM((2*FREQ,D),F32)],
        compiler_params=pltpu.CompilerParams(vmem_limit_bytes=60*1024*1024, dimension_semantics=("arbitrary",)),
        name="encode",
    )(*args)


def shards(
    feature_maps,
    down_weight,
    conv_taps,
    mlp_in,
    mlp_out,
    layer_scale,
    qkv_weight,
    out_weight,
    tile_slide,
    tile_pos,
    slide_len,
):
    slide_count = lax.axis_size("slide")
    ctx_count = lax.axis_size("ctx")
    device_count = slide_count * ctx_count
    capacity = (SEQ_DEV + device_count - 1) // device_count
    buffer_rows = device_count * capacity
    model_width = qkv_weight.shape[1]
    tiles_here = feature_maps.shape[0]
    embeds = encode(feature_maps, down_weight, conv_taps, mlp_in, mlp_out, layer_scale)
    owner_index = tile_slide * ctx_count + tile_pos // SEQ_DEV
    tile_order = jnp.arange(tiles_here, dtype=jnp.int32)
    earlier = (owner_index[None, :] == owner_index[:, None]) & (
        tile_order[None, :] < tile_order[:, None]
    )
    tile_rank = jnp.sum(earlier.astype(jnp.int32), axis=1)
    target_row = owner_index * capacity + tile_rank
    placing = jnp.arange(buffer_rows, dtype=jnp.int32)[:, None] == target_row[None, :]
    outgoing = jnp.dot(
        placing.astype(jnp.bfloat16), embeds, preferred_element_type=jnp.float32
    ).astype(jnp.bfloat16)
    local_slot = tile_pos % SEQ_DEV
    slot_sent = jnp.sum(jnp.where(placing, local_slot[None, :] + 1, 0), axis=1) - 1
    slot_sent = jnp.where(slot_sent < 0, SEQ_DEV, slot_sent)
    arrived, arrived_slot = (
        lax.all_to_all(outgoing, ("slide", "ctx"), split_axis=0, concat_axis=0, tiled=True),
        lax.all_to_all(slot_sent, ("slide", "ctx"), split_axis=0, concat_axis=0, tiled=True),
    )
    position = jnp.arange(SEQ_DEV, dtype=jnp.int32)
    picking = (position[:, None] == arrived_slot[None, :]).astype(jnp.bfloat16)
    slot_rows = jnp.dot(picking, arrived, preferred_element_type=jnp.float32).astype(jnp.bfloat16)
    stream = slot_rows.astype(jnp.float32)
    length = slide_len[lax.axis_index("slide")]
    query_pos = lax.axis_index("ctx") * SEQ_DEV + position
    score_scale = HEAD_DIM ** (-0.5)
    lnorm = layer_norm(stream).astype(jnp.bfloat16)
    query_weight = qkv_weight[0, :, :model_width]
    key_weight = qkv_weight[0, :, model_width:]
    queries = jnp.dot(lnorm, query_weight, preferred_element_type=jnp.float32).astype(jnp.bfloat16)
    queries = queries.reshape(SEQ_DEV, HEADS, HEAD_DIM)
    local_kv = jnp.dot(lnorm, key_weight, preferred_element_type=jnp.float32).astype(jnp.bfloat16)
    key_rows = lax.all_gather(local_kv, "ctx", axis=0, tiled=True)
    running_max = jnp.full((HEADS, SEQ_DEV), FAR_NEGATIVE, jnp.float32)
    row_count = key_rows.shape[0]
    keys_part = key_rows[:, :model_width].reshape(row_count, HEADS, HEAD_DIM)
    values_part = key_rows[:, model_width:].reshape(row_count, HEADS, HEAD_DIM)
    scores = (
        jnp.einsum("qhe,khe->hqk", queries, keys_part, preferred_element_type=jnp.float32)
        * score_scale
    )
    included = jnp.arange(row_count, dtype=jnp.int32) < length
    scores = jnp.where(included[None, None, :], scores, FAR_NEGATIVE)
    new_max = jnp.maximum(running_max, jnp.max(scores, axis=-1))
    weights = jnp.where(included[None, None, :], jnp.exp(scores - new_max[:, :, None]), 0.0)
    denom_sum = jnp.sum(weights, axis=-1)
    accum = jnp.einsum(
        "hqk,khe->hqe",
        weights.astype(jnp.bfloat16),
        values_part,
        preferred_element_type=jnp.float32,
    )
    folded = (new_max, denom_sum, accum)
    running_max, denom_sum, accum = folded
    attended = (accum / denom_sum[:, :, None]).transpose(1, 0, 2).reshape(SEQ_DEV, model_width)
    attended = attended.astype(jnp.bfloat16)
    stream = stream + jnp.dot(attended, out_weight[0], preferred_element_type=jnp.float32)
    valid_rows = query_pos < length
    return jnp.where(valid_rows[:, None], stream, 0.0).astype(jnp.bfloat16)


def solution(mesh):
    return jax.shard_map(
        shards,
        mesh=mesh,
        in_specs=(
            P(("slide", "ctx"), None, None, None),
            P(),
            P(),
            P(),
            P(),
            P(),
            P(),
            P(),
            P(("slide", "ctx")),
            P(("slide", "ctx")),
            P(),
        ),
        out_specs=P(("slide", "ctx"), None),
        check_vma=False,
    )
```

```python
import functools

import jax
import jax.numpy as jnp
import numpy as np
from jax import lax
from jax.experimental import pallas as pl
from jax.experimental.pallas import tpu as pltpu
from jax.sharding import PartitionSpec as P

HEADS = 12
HEAD_DIM = 64
SEQ_DEV = 192
META = 128
NORM_EPS = 1e-06
FAR_NEGATIVE = -1e30
F32=jnp.float32; BF=jnp.bfloat16
FREQ=64
C0,C1,C2=0.796875,0.03759765625,-0.000457763671875

def tables(side, ks):
    reach=ks//2; n=side+reach
    half=[(0,0)]+[(0,l) for l in range(1,n//2+1)]+[(k,l) for k in range(1,n//2+1) for l in range(n)]
    k=np.array([a for a,_ in half]); l=np.array([b for _,b in half])
    pos=np.arange(side*side); i,j=pos//side,pos%side
    th=2*np.pi*(np.outer(k,i)+np.outer(l,j))/n
    fwd=np.zeros((2*FREQ,side*side)); fwd[:len(half)]=np.cos(th); fwd[FREQ:FREQ+len(half)]=-np.sin(th)
    a=np.arange(ks*ks)//ks-reach; b=np.arange(ks*ks)%ks-reach
    ph=2*np.pi*(np.outer(k,a)+np.outer(l,b))/n
    s=np.where(np.arange(len(half))==0,1.0,2.0)[:,None]/(n*n)
    tap=np.zeros((2*FREQ,ks*ks)); tap[:len(half)]=s*np.cos(ph); tap[FREQ:FREQ+len(half)]=s*np.sin(ph)
    inv=fwd.T.copy()
    perm=np.zeros((4*side*side,4*side*side))
    for dy in range(2):
        for dx in range(2):
            for ii in range(side):
                for jj in range(side):
                    perm[(dy*2+dx)*side*side+ii*side+jj,(2*ii+dy)*2*side+2*jj+dx]=1
    hi=tap.astype(jnp.bfloat16).astype(np.float64)
    return fwd, inv, np.concatenate([hi,tap-hi]), perm

def rows_norm(x):
    c=x-jnp.mean(x,axis=-1,keepdims=True)
    return c*lax.rsqrt(jnp.mean(c*c,axis=-1,keepdims=True)+NORM_EPS)

def gelu_sums(h, tiles, rows):
    b=h.astype(BF)
    w=jnp.minimum(b*b, jnp.asarray(50.0,BF))
    p=jnp.asarray(C0,BF)+w*(jnp.asarray(C1,BF)+jnp.asarray(C2,BF)*w)
    e=b+b*jnp.tanh(b*p)
    e=e.reshape(tiles,rows//16,16,h.shape[1])
    parts=[e[:,i] for i in range(rows//16)]
    while len(parts)>1:
        parts=[a+c for a,c in zip(parts[::2],parts[1::2])]
    s=parts[0].astype(F32).reshape(tiles,2,8,h.shape[1])
    return (s[:,0]+s[:,1]).reshape(tiles*8,h.shape[1])

def meta_cols(slides, places, count, blocks):
    row=lax.broadcasted_iota(jnp.int32,(count,META),0)
    lane=lax.broadcasted_iota(jnp.int32,(count,META),1)
    cols=jnp.zeros((count,META),jnp.int32)
    for t in range(count):
        place=places[t]
        block=jnp.int32(0)
        for edge in range(1,blocks):
            block=block+(place>=edge*SEQ_DEV).astype(jnp.int32)
        vals=jnp.where(lane==0,slides[t],jnp.where(lane==1,block,place-block*SEQ_DEV))
        cols=jnp.where((row==t)&(lane<3),vals,cols)
    return cols.astype(F32).astype(BF)

def kernel(G, side, blocks, NC, steps, feat, down_h, taps, win_h, wout_h, scale, slides, places, fwd, inv, taptab, perm, out,
           patches, red, sn_a, sn_b, psum, pool, khat, down, win, wout, hbuf, sems):
    step=pl.program_id(0)
    S=side*side
    C=feat.shape[-1]; D=down.shape[1]; M=win.shape[1]; T=out.shape[0]
    cp_down=pltpu.make_async_copy(down_h,down,sems.at[0])
    cp_in=pltpu.make_async_copy(win_h,win,sems.at[1])
    cp_out=pltpu.make_async_copy(wout_h,wout,sems.at[2])

    def a1(t):
        xp=jnp.dot(perm[...],feat[t],preferred_element_type=F32)
        n=rows_norm(xp).astype(BF)
        for q in range(4):
            patches[t*S:(t+1)*S, q*C:(q+1)*C]=n[q*S:(q+1)*S]
    def a2(c, w):
        red[:,c*w:(c+1)*w]=jnp.dot(patches[...],down[:,c*w:(c+1)*w],preferred_element_type=F32).astype(BF)
    def a3(t):
        f=jnp.dot(fwd[...],red[t*S:(t+1)*S,:],preferred_element_type=F32)
        pool[pl.ds(step*G+t,1),:]=f[0:1]*(1.0/S)
        fr,fi=f[:FREQ],f[FREQ:]
        kr,ki=khat[:FREQ,:],khat[FREQ:,:]
        g=jnp.concatenate([fr*kr-fi*ki, fr*ki+fi*kr],axis=0).astype(BF)
        sp=jnp.dot(inv[...],g,preferred_element_type=F32)
        sn_a[t*S:(t+1)*S,:]=rows_norm(sp).astype(BF)
    def b1(c):
        hbuf[c%2]=jnp.dot(sn_b[...],win[:,c*NC:(c+1)*NC],preferred_element_type=F32).astype(hbuf.dtype)
    def b2(c):
        psum[pl.ds(pl.multiple_of((step-1)*G*8,G*8),G*8), c*NC:(c+1)*NC]=gelu_sums(hbuf[c%2],G,S).astype(BF)
    a_items=[(lambda t=t:a1(t)) for t in range(G)]+[(lambda c=c:a2(c,256)) for c in range(D//256)]+[(lambda t=t:a3(t)) for t in range(G)]
    b_items=[]
    for c in range(M//NC+1):
        def item(c=c):
            if c<M//NC: b1(c)
            if c>0: b2(c-1)
        b_items.append(item)
    def keep():
        sn_b[...]=sn_a[...]

    @pl.when(step==0)
    def _():
        cp_down.start(); cp_in.start(); cp_out.start()
        t2=jnp.dot(taptab[...],taps[...],preferred_element_type=F32)
        khat[...]=t2[:2*FREQ]+t2[2*FREQ:]
        for t in range(G): a1(t)
        cp_down.wait()
        for f in a_items[G:]: f()
        cp_in.wait()
        keep()
    @pl.when((step>0)&(step<steps))
    def _():
        na,nb=len(a_items),len(b_items)
        done=0
        for i,f in enumerate(b_items):
            f()
            upto=(i+1)*na//nb
            for g in a_items[done:upto]: g()
            done=upto
        keep()
    @pl.when(step==steps)
    def _():
        for f in b_items: f()
        cp_out.wait()
        z=jnp.dot(psum[...],wout[...],preferred_element_type=F32)
        z=z.reshape(z.shape[0]//8,8,D).sum(axis=1)*(0.5/S)
        out[:,:D]=rows_norm(pool[...]+scale[...].reshape(1,D)*z).astype(BF)
        out[:,D:]=meta_cols(slides,places,T,blocks)

def encode(feature_maps, down, taps, win, wout, scale, tile_slide, tile_pos, G=8, NC=256, hb=BF):
    T,H,W,C=feature_maps.shape
    side=H//2; S=side*side; D=down.shape[1]; M=win.shape[1]; ks=int(round(taps.shape[0]**.5))
    fwd,inv,tt,perm=tables(side,ks)
    blocks=lax.axis_size("ctx")
    steps=T//G
    full=lambda a: pl.BlockSpec(a.shape,lambda s:(0,)*a.ndim,pipeline_mode=pl.Buffered(1))
    hbm=pl.BlockSpec(memory_space=pl.ANY); smem=pl.BlockSpec(memory_space=pltpu.SMEM)
    tabs=[jnp.asarray(a,BF) for a in (fwd,inv,tt,perm)]
    r=pl.pallas_call(
        functools.partial(kernel,G,side,blocks,NC,steps),
        grid=(steps+1,),
        in_specs=[pl.BlockSpec((G,H*W,C),lambda s:(jnp.minimum(s,steps-1),0,0)),hbm,full(taps),hbm,hbm,full(scale),smem,smem]+[full(a) for a in tabs],
        out_specs=pl.BlockSpec((T,D+META),lambda s:(0,0)),
        out_shape=jax.ShapeDtypeStruct((T,D+META),BF),
        scratch_shapes=[pltpu.VMEM((G*S,4*C),BF),pltpu.VMEM((G*S,D),BF),pltpu.VMEM((G*S,D),BF),pltpu.VMEM((G*S,D),BF),
                        pltpu.VMEM((T*8,M),BF),pltpu.VMEM((T,D),F32),pltpu.VMEM((2*FREQ,D),F32),
                        pltpu.VMEM(down.shape,BF),pltpu.VMEM(win.shape,BF),pltpu.VMEM(wout.shape,BF),
                        pltpu.VMEM((2,G*S,NC),hb),pltpu.SemaphoreType.DMA((3,))],
        compiler_params=pltpu.CompilerParams(vmem_limit_bytes=60*1024*1024, dimension_semantics=("arbitrary",)),
        name="encode",
    )(feature_maps.reshape(T,H*W,C),down,taps,win,wout,scale,tile_slide,tile_pos,*tabs)
    return r


def gather_rows(rows, count):
    span_left = count
    while span_left > 1:
        span = 4 if span_left >= 4 else 2
        unit = span_left // span
        parts = [rows]
        for mask in range(1, span):
            pairs = [(dev, dev ^ (mask * unit)) for dev in range(count)]
            parts.append(lax.ppermute(rows, ("slide", "ctx"), pairs))
        span_left = unit
        if span_left > 1:
            rows = jnp.concatenate(parts, axis=0)
    return parts


def attend_kernel(part_count, chunk, *refs):
    parts = refs[:part_count]
    qkv, wout, lens, out, keyvals, bias, attended = refs[part_count:]
    D = wout.shape[0]
    rows_dev = out.shape[0]
    part_rows = parts[0].shape[0]
    my_slide = lax.axis_index("slide")
    my_ctx = lax.axis_index("ctx")
    length = lens[my_slide]
    slide_f = my_slide.astype(F32)
    ctx_f = my_ctx.astype(F32)
    pick_lane = (
        lax.broadcasted_iota(jnp.int32, (8, META), 0) == lax.broadcasted_iota(jnp.int32, (8, META), 1)
    ).astype(BF)
    slot = lax.broadcasted_iota(jnp.int32, (rows_dev, 1), 0).astype(F32)
    stream = jnp.zeros((rows_dev, D), F32)
    for index, part in enumerate(parts):
        ids = lax.dot_general(
            pick_lane, part[:, D:], (((1,), (1,)), ((), ())), preferred_element_type=F32
        )
        here = ids[0:1] == slide_f
        place = ids[1:2] * float(rows_dev) + ids[2:3]
        included = here & (place < length.astype(F32))
        bias[:, index * part_rows : (index + 1) * part_rows] = jnp.where(included, 0.0, FAR_NEGATIVE)
        target = jnp.where(here & (ids[1:2] == ctx_f), ids[2:3], -1.0)
        picking = (slot == target).astype(BF)
        stream = stream + jnp.dot(picking, part[:, :D], preferred_element_type=F32)
        for start in range(0, part_rows, chunk):
            lnorm = rows_norm(part[start : start + chunk, :D].astype(F32)).astype(BF)
            keyvals[index * part_rows + start : index * part_rows + start + chunk, :] = jnp.dot(
                lnorm, qkv[:, D:], preferred_element_type=F32
            ).astype(BF)
    lnorm = rows_norm(stream).astype(BF)
    queries = jnp.dot(lnorm, qkv[:, :D], preferred_element_type=F32).astype(BF)
    lane = lax.broadcasted_iota(jnp.int32, (1, 2 * HEAD_DIM), 1)
    low = lane < HEAD_DIM
    scale = jnp.asarray(HEAD_DIM**-0.5, BF)
    for pair in range(HEADS // 2):
        cols = slice(pair * 2 * HEAD_DIM, (pair + 1) * 2 * HEAD_DIM)
        vcols = slice(D + pair * 2 * HEAD_DIM, D + (pair + 1) * 2 * HEAD_DIM)
        both = queries[:, cols] * scale
        zero = jnp.zeros_like(both)
        stacked = jnp.concatenate([jnp.where(low, both, zero), jnp.where(low, zero, both)], axis=0)
        scores = lax.dot_general(
            stacked, keyvals[:, cols], (((1,), (1,)), ((), ())), preferred_element_type=F32
        )
        scores = scores + bias[...]
        weights = jnp.exp(scores - jnp.max(scores, axis=-1, keepdims=True))
        denom = jnp.sum(weights, axis=-1, keepdims=True)
        mixed = jnp.dot(weights.astype(BF), keyvals[:, vcols], preferred_element_type=F32) / denom
        attended[:, cols] = jnp.where(low, mixed[:rows_dev], mixed[rows_dev:]).astype(BF)
    stream = stream + jnp.dot(attended[...], wout[...], preferred_element_type=F32)
    valid = (slot + ctx_f * float(rows_dev)) < length.astype(F32)
    out[...] = jnp.where(valid, stream, 0.0).astype(BF)


def attend(parts, qkv, wout, lens):
    D = wout.shape[0]
    total = len(parts) * parts[0].shape[0]
    chunk = min(256, parts[0].shape[0])
    vmem = pl.BlockSpec(memory_space=pltpu.VMEM)
    return pl.pallas_call(
        functools.partial(attend_kernel, len(parts), chunk),
        in_specs=[vmem] * (len(parts) + 2) + [pl.BlockSpec(memory_space=pltpu.SMEM)],
        out_specs=vmem,
        out_shape=jax.ShapeDtypeStruct((SEQ_DEV, D), BF),
        scratch_shapes=[
            pltpu.VMEM((total, 2 * D), BF),
            pltpu.VMEM((1, total), F32),
            pltpu.VMEM((SEQ_DEV, D), BF),
        ],
        compiler_params=pltpu.CompilerParams(vmem_limit_bytes=56 * 1024 * 1024),
        name="attend",
    )(*parts, qkv, wout, lens)


def shards(
    feature_maps,
    down_weight,
    conv_taps,
    mlp_in,
    mlp_out,
    layer_scale,
    qkv_weight,
    out_weight,
    tile_slide,
    tile_pos,
    slide_len,
):
    device_count = lax.axis_size("slide") * lax.axis_size("ctx")
    rows = encode(
        feature_maps, down_weight, conv_taps, mlp_in, mlp_out, layer_scale, tile_slide, tile_pos
    )
    parts = gather_rows(rows, device_count)
    return attend(parts, qkv_weight[0], out_weight[0], slide_len)


def solution(mesh):
    return jax.shard_map(
        shards,
        mesh=mesh,
        in_specs=(
            P(("slide", "ctx"), None, None, None),
            P(),
            P(),
            P(),
            P(),
            P(),
            P(),
            P(),
            P(("slide", "ctx")),
            P(("slide", "ctx")),
            P(),
        ),
        out_specs=P(("slide", "ctx"), None),
        check_vma=False,
    )
```

```python
import functools

import jax
import jax.numpy as jnp
import numpy as np
from jax import lax
from jax.experimental import pallas as pl
from jax.experimental.pallas import tpu as pltpu
from jax.sharding import PartitionSpec as P

HEADS = 12
HEAD_DIM = 64
SEQ_DEV = 192
META = 128
NORM_EPS = 1e-06
FAR_NEGATIVE = -1e30
F32=jnp.float32; BF=jnp.bfloat16
FREQ=64
FT,IT=4,2
VM=58
C0,C1,C2=0.796875,0.03759765625,-0.000457763671875

def tables(side, ks):
    reach=ks//2; n=side+reach
    half=[(0,0)]+[(0,l) for l in range(1,n//2+1)]+[(k,l) for k in range(1,n//2+1) for l in range(n)]
    k=np.array([a for a,_ in half]); l=np.array([b for _,b in half])
    pos=np.arange(side*side); i,j=pos//side,pos%side
    th=2*np.pi*(np.outer(k,i)+np.outer(l,j))/n
    fwd=np.zeros((2*FREQ,side*side)); fwd[:len(half)]=np.cos(th); fwd[FREQ:FREQ+len(half)]=-np.sin(th)
    a=np.arange(ks*ks)//ks-reach; b=np.arange(ks*ks)%ks-reach
    ph=2*np.pi*(np.outer(k,a)+np.outer(l,b))/n
    s=np.where(np.arange(len(half))==0,1.0,2.0)[:,None]/(n*n)
    tap=np.zeros((2*FREQ,ks*ks)); tap[:len(half)]=s*np.cos(ph); tap[FREQ:FREQ+len(half)]=s*np.sin(ph)
    inv=fwd.T.copy()
    hi=tap.astype(jnp.bfloat16).astype(np.float64)
    return fwd, inv, np.concatenate([hi,tap-hi])

def rows_norm(x):
    c=x-jnp.mean(x,axis=-1,keepdims=True)
    return c*lax.rsqrt(jnp.mean(c*c,axis=-1,keepdims=True)+NORM_EPS)

def gelu_sums(h, tiles, rows):
    b=h.astype(BF)
    w=jnp.minimum(b*b, jnp.asarray(50.0,BF))
    p=jnp.asarray(C0,BF)+w*(jnp.asarray(C1,BF)+jnp.asarray(C2,BF)*w)
    e=b+b*jnp.tanh(b*p)
    e=e.reshape(tiles,rows//16,16,h.shape[1])
    parts=[e[:,i] for i in range(rows//16)]
    while len(parts)>1:
        parts=[a+c for a,c in zip(parts[::2],parts[1::2])]
    s=parts[0].astype(F32).reshape(tiles,2,8,h.shape[1])
    return (s[:,0]+s[:,1]).reshape(tiles*8,h.shape[1])

def meta_cols(slides, places, count, blocks):
    row=lax.broadcasted_iota(jnp.int32,(count,META),0)
    lane=lax.broadcasted_iota(jnp.int32,(count,META),1)
    cols=jnp.zeros((count,META),jnp.int32)
    for t in range(count):
        place=places[t]
        block=jnp.int32(0)
        for edge in range(1,blocks):
            block=block+(place>=edge*SEQ_DEV).astype(jnp.int32)
        vals=jnp.where(lane==0,slides[t],jnp.where(lane==1,block,place-block*SEQ_DEV))
        cols=jnp.where((row==t)&(lane<3),vals,cols)
    return cols.astype(F32).astype(BF)

def kernel(G, side, blocks, NC, steps, feat, down_h, win_h, wout_h, taps_h, fwd_h, inv_h, taptab_h, scale, slides, places, out,
           patches, red, sn_a, sn_b, psum, pool, khat, hbuf, down, win, wout, taps, fwd, inv, taptab, normed, sems):
    step=pl.program_id(0)
    S=side*side
    C=feat.shape[-1]; D=down.shape[1]; M=win.shape[1]; T=out.shape[0]
    def copy(src,dst,index):
        return pltpu.make_async_copy(src,dst,sems.at[index])
    cp_down=copy(down_h,down,0)
    cp_in=copy(win_h,win,1)
    cp_out=copy(wout_h,wout,2)
    cp_small=[copy(a,b,3+i) for i,(a,b) in enumerate([(taps_h,taps),(taptab_h,taptab),(fwd_h,fwd),(inv_h,inv)])]

    def a1(t):
        slot=t%2
        full=rows_norm(feat[t].astype(F32))
        for l in range(C//128):
            normed[slot*(C//128)+l]=full[:,l*128:(l+1)*128]
        for l in range(C//128):
            held=slot*(C//128)+l
            for dy in range(2):
                for dx in range(2):
                    rows=[normed[held,pl.ds((2*i+dy)*2*side+dx,side,stride=2),:] for i in range(side)]
                    at=(dy*2+dx)*C+l*128
                    patches[t*S:(t+1)*S, at:at+128]=jnp.concatenate(rows,axis=0).astype(BF)
    def a2(c, w):
        red[:,c*w:(c+1)*w]=jnp.dot(patches[...],down[:,c*w:(c+1)*w],preferred_element_type=F32).astype(BF)
    def a3(t):
        f=jnp.dot(fwd[...],red[t*S:(t+FT)*S,:],preferred_element_type=F32)
        kr,ki=khat[:FREQ,:],khat[FREQ:,:]
        gs=[]
        for u in range(FT):
            fr,fi=f[2*u*FREQ:(2*u+1)*FREQ],f[(2*u+1)*FREQ:(2*u+2)*FREQ]
            pool[pl.ds(step*G+t+u,1),:]=fr[0:1]*(1.0/S)
            gs+=[(fr*kr-fi*ki).astype(BF),(fr*ki+fi*kr).astype(BF)]
        for u in range(0,FT,IT):
            g=jnp.concatenate(gs[2*u:2*(u+IT)],axis=0)
            sp=jnp.dot(inv[...],g,preferred_element_type=F32)
            sn_a[(t+u)*S:(t+u+IT)*S,:]=rows_norm(sp).astype(BF)
    def b1(c):
        hbuf[c%2]=jnp.dot(sn_b[...],win[:,c*NC:(c+1)*NC],preferred_element_type=F32).astype(hbuf.dtype)
    def b2(c):
        psum[pl.ds(pl.multiple_of((step-1)*G*8,G*8),G*8), c*NC:(c+1)*NC]=gelu_sums(hbuf[c%2],G,S).astype(BF)
    a_items=[(lambda t=t:a1(t)) for t in range(G)]+[(lambda c=c:a2(c,256)) for c in range(D//256)]+[(lambda t=t:a3(t)) for t in range(0,G,FT)]
    b_items=[]
    for c in range(M//NC+1):
        def item(c=c):
            if c<M//NC: b1(c)
            if c>0: b2(c-1)
        b_items.append(item)
    def keep():
        sn_b[...]=sn_a[...]

    @pl.when(step==0)
    def _():
        cp_down.start()
        for cp in cp_small: cp.start()
        cp_in.start(); cp_out.start()
        out[:,D:]=meta_cols(slides,places,T,blocks)
        for t in range(G): a1(t)
        for cp in cp_small: cp.wait()
        t2=jnp.dot(taptab[...],taps[...],preferred_element_type=F32)
        khat[...]=t2[:2*FREQ]+t2[2*FREQ:]
        cp_down.wait()
        for f in a_items[G:]: f()
        cp_in.wait()
        keep()
    @pl.when((step>0)&(step<steps))
    def _():
        na,nb=len(a_items),len(b_items)
        done=0
        for i,f in enumerate(b_items):
            f()
            upto=(i+1)*na//nb
            for g in a_items[done:upto]: g()
            done=upto
        keep()
    @pl.when(step==steps)
    def _():
        for f in b_items: f()
        cp_out.wait()
        z=jnp.dot(psum[...],wout[...],preferred_element_type=F32)
        z=z.reshape(z.shape[0]//8,8,D).sum(axis=1)*(0.5/S)
        out[:,:D]=rows_norm(pool[...]+scale[...].reshape(1,D)*z).astype(BF)

def encode(feature_maps, down, taps, win, wout, scale, tile_slide, tile_pos, G=8, NC=256, hb=BF):
    T,H,W,C=feature_maps.shape
    side=H//2; S=side*side; D=down.shape[1]; M=win.shape[1]; ks=int(round(taps.shape[0]**.5))
    fwd,inv,tt=tables(side,ks)
    blocks=lax.axis_size("ctx")
    steps=T//G


    fwd=np.kron(np.eye(FT),fwd); inv=np.kron(np.eye(IT),inv)
    full=lambda a: pl.BlockSpec(a.shape,lambda s:(0,)*a.ndim,pipeline_mode=pl.Buffered(1))
    hbm=pl.BlockSpec(memory_space=pltpu.HBM); smem=pl.BlockSpec(memory_space=pltpu.SMEM)
    held=[down,win,wout,taps]+[jnp.asarray(a,BF) for a in (fwd,inv,tt)]
    r=pl.pallas_call(
        functools.partial(kernel,G,side,blocks,NC,steps),
        grid=(steps+1,),
        in_specs=[pl.BlockSpec((G,H*W,C),lambda s:(jnp.minimum(s,steps-1),0,0))]+[hbm]*7+[full(scale),smem,smem],
        out_specs=pl.BlockSpec((T,D+META),lambda s:(0,0)),
        out_shape=pltpu.VMEM((T,D+META),BF),
        scratch_shapes=[pltpu.VMEM((G*S,4*C),BF),pltpu.VMEM((G*S,D),BF),pltpu.VMEM((G*S,D),BF),pltpu.VMEM((G*S,D),BF),
                        pltpu.VMEM((T*8,M),BF),pltpu.VMEM((T,D),F32),pltpu.VMEM((2*FREQ,D),F32),
                        pltpu.VMEM((2,G*S,NC),hb)]+[pltpu.VMEM(a.shape,BF) for a in held]+[pltpu.VMEM((2*(C//128),H*W,128),F32)]+[pltpu.SemaphoreType.DMA((len(held),))],
        compiler_params=pltpu.CompilerParams(vmem_limit_bytes=VM*1024*1024, dimension_semantics=("arbitrary",)),
        name="encode",
    )(feature_maps.reshape(T,H*W,C),*held,scale,tile_slide,tile_pos)
    return r


def gather_rows(rows, count):
    span_left = count
    while span_left > 1:
        span = 4 if span_left >= 4 else 2
        unit = span_left // span
        parts = [rows]
        for mask in range(1, span):
            pairs = [(dev, dev ^ (mask * unit)) for dev in range(count)]
            parts.append(lax.ppermute(rows, ("slide", "ctx"), pairs))
        span_left = unit
        if span_left > 1:
            rows = jnp.concatenate(parts, axis=0)
    return parts


def take_part(part, qkv, chunk, rows_dev, my_slide, my_ctx, keyvals):
    D = part.shape[1] - META
    pick_lane = (
        lax.broadcasted_iota(jnp.int32, (8, META), 0) == lax.broadcasted_iota(jnp.int32, (8, META), 1)
    ).astype(BF)
    ids = lax.dot_general(
        pick_lane, part[:, D:], (((1,), (1,)), ((), ())), preferred_element_type=F32
    )
    here = ids[0:1] == my_slide.astype(F32)
    target = jnp.where(here & (ids[1:2] == my_ctx.astype(F32)), ids[2:3], -1.0)
    slot = lax.broadcasted_iota(jnp.int32, (rows_dev, 1), 0).astype(F32)
    picking = (slot == target).astype(BF)
    for start in range(0, part.shape[0], chunk):
        rows = slice(start, start + chunk)
        lnorm = rows_norm(part[rows, :D].astype(F32)).astype(BF)
        keyvals[rows, :] = jnp.dot(lnorm, qkv[:, D:], preferred_element_type=F32).astype(BF)
    picked = jnp.dot(picking, part[:, :D], preferred_element_type=F32)
    return picked, here, ids[1:2] * float(rows_dev) + ids[2:3]


def project_kernel(chunk, part, qkv, keyvals, picked):
    my_slide, my_ctx = lax.axis_index("slide"), lax.axis_index("ctx")
    rows, _, _ = take_part(part, qkv, chunk, picked.shape[0], my_slide, my_ctx, keyvals)
    picked[...] = rows.astype(BF)


def attend_kernel(chunk, near, far, near_keyvals, near_picked, qkv, wout, lens, out, far_keyvals, attended):
    D = wout.shape[0]
    rows_dev = out.shape[0]
    my_slide, my_ctx = lax.axis_index("slide"), lax.axis_index("ctx")
    length = lens[my_slide].astype(F32)
    pick_lane = (
        lax.broadcasted_iota(jnp.int32, (8, META), 0) == lax.broadcasted_iota(jnp.int32, (8, META), 1)
    ).astype(BF)
    ids = lax.dot_general(
        pick_lane, near[:, D:], (((1,), (1,)), ((), ())), preferred_element_type=F32
    )
    near_here = ids[0:1] == my_slide.astype(F32)
    near_place = ids[1:2] * float(rows_dev) + ids[2:3]
    picked, far_here, far_place = take_part(far, qkv, chunk, rows_dev, my_slide, my_ctx, far_keyvals)
    here = jnp.concatenate([near_here, far_here], axis=1)
    place = jnp.concatenate([near_place, far_place], axis=1)
    bias = jnp.where(here & (place < length), 0.0, FAR_NEGATIVE)
    stream = near_picked[...].astype(F32) + picked
    lnorm = rows_norm(stream).astype(BF)
    queries = jnp.dot(lnorm, qkv[:, :D], preferred_element_type=F32).astype(BF)
    lane = lax.broadcasted_iota(jnp.int32, (1, 2 * HEAD_DIM), 1)
    low = lane < HEAD_DIM
    scale = jnp.asarray(HEAD_DIM**-0.5, BF)
    half = near.shape[0]
    ones = jnp.ones((half, 2 * HEAD_DIM), BF)
    for pair in range(HEADS // 2):
        cols = slice(pair * 2 * HEAD_DIM, (pair + 1) * 2 * HEAD_DIM)
        vcols = slice(D + pair * 2 * HEAD_DIM, D + (pair + 1) * 2 * HEAD_DIM)
        both = queries[:, cols] * scale
        zero = jnp.zeros_like(both)
        stacked = jnp.concatenate([jnp.where(low, both, zero), jnp.where(low, zero, both)], axis=0)
        scores = [
            lax.dot_general(stacked, held[:, cols], (((1,), (1,)), ((), ())), preferred_element_type=F32)
            for held in (near_keyvals, far_keyvals)
        ]
        scores = [scores[0] + bias[:, :half], scores[1] + bias[:, half:]]
        peak = jnp.max(jnp.maximum(scores[0], scores[1]), axis=-1, keepdims=True)
        mixed = jnp.zeros((2 * rows_dev, 4 * HEAD_DIM), F32)
        for part, held in zip(scores, (near_keyvals, far_keyvals)):
            values = jnp.concatenate([held[:, vcols], ones], axis=1)
            mixed = mixed + jnp.dot(jnp.exp((part - peak).astype(BF)), values, preferred_element_type=F32)
        mixed = mixed[:, : 2 * HEAD_DIM] / mixed[:, 2 * HEAD_DIM :]
        attended[:, cols] = jnp.where(low, mixed[:rows_dev], mixed[rows_dev:]).astype(BF)
    stream = stream + jnp.dot(attended[...], wout[...], preferred_element_type=F32)
    slot = lax.broadcasted_iota(jnp.int32, (rows_dev, 1), 0).astype(F32)
    valid = (slot + my_ctx.astype(F32) * float(rows_dev)) < length
    out[...] = jnp.where(valid, stream, 0.0).astype(BF)


VMEM_SPEC = pl.BlockSpec(memory_space=pltpu.VMEM)


def project(part, qkv):
    rows, width = part.shape
    D = width - META
    return pl.pallas_call(
        functools.partial(project_kernel, min(256, rows)),
        in_specs=[VMEM_SPEC] * 2,
        out_specs=[VMEM_SPEC] * 2,
        out_shape=[pltpu.VMEM((rows, 2 * D), BF), pltpu.VMEM((SEQ_DEV, D), BF)],
        compiler_params=pltpu.CompilerParams(vmem_limit_bytes=24 * 1024 * 1024),
        cost_estimate=pl.CostEstimate(flops=4 * rows * D * D, bytes_accessed=8 * rows * D, transcendentals=rows),
        name="project",
    )(part, qkv)


def attend(near, far, keyvals, picked, qkv, wout, lens):
    D = wout.shape[0]
    rows = far.shape[0]
    return pl.pallas_call(
        functools.partial(attend_kernel, min(256, rows)),
        in_specs=[VMEM_SPEC] * 6 + [pl.BlockSpec(memory_space=pltpu.SMEM)],
        out_specs=VMEM_SPEC,
        out_shape=jax.ShapeDtypeStruct((SEQ_DEV, D), BF),
        scratch_shapes=[pltpu.VMEM((rows, 2 * D), BF), pltpu.VMEM((SEQ_DEV, D), BF)],
        compiler_params=pltpu.CompilerParams(vmem_limit_bytes=24 * 1024 * 1024),
        name="attend",
    )(near, far, keyvals, picked, qkv, wout, lens)


def shards(
    feature_maps,
    down_weight,
    conv_taps,
    mlp_in,
    mlp_out,
    layer_scale,
    qkv_weight,
    out_weight,
    tile_slide,
    tile_pos,
    slide_len,
):
    device_count = lax.axis_size("slide") * lax.axis_size("ctx")
    rows = encode(
        feature_maps, down_weight, conv_taps, mlp_in, mlp_out, layer_scale, tile_slide, tile_pos
    )
    near, far = gather_rows(rows, device_count)
    keyvals, picked = project(near, qkv_weight[0])
    return attend(near, far, keyvals, picked, qkv_weight[0], out_weight[0], slide_len)


def solution(mesh):
    return jax.shard_map(
        shards,
        mesh=mesh,
        in_specs=(
            P(("slide", "ctx"), None, None, None),
            P(),
            P(),
            P(),
            P(),
            P(),
            P(),
            P(),
            P(("slide", "ctx")),
            P(("slide", "ctx")),
            P(),
        ),
        out_specs=P(("slide", "ctx"), None),
        check_vma=False,
    )
```
